32 devices in a mesh: layer: 4 (over z), rep: 2 (over core), row: 2 (over x), col: 2 (over y).
Axes of the slice: x: 2, y: 2, z: 4, core: 2. Of those that a mesh axis runs over, the one named last changes fastest.
Arguments:
- iterate: bfloat16 [14336, 8192], P(('layer', 'row'), ('rep', 'col')), parts along dimension 0, may hold values from -0.03125 to 0.03125
Outputs:
- next_iterate: bfloat16 [14336, 8192], P(('layer', 'row'), ('rep', 'col')), parts along dimension 0
The draws below stay inside these ranges and needn't reach their ends.
There are 4 independent parts, one for each index of `layer`. The reference program is written for one: setup_inputs(seed, part) draws one part's arguments, and reference() takes and returns one part's arrays. A program takes and returns all parts, laid end to end along the dimension named above; each array names one. Nothing has to cross between parts.
All inputs are finite; a program needn't handle non-finite values.
Results may differ from the reference program's by a relative error of at most 0.017.
Values may be sent and summed in bfloat16 or wider, within the bound.
No kernel may reach another device: no remote copies, remote signals or barrier semaphores. Data moves between devices by JAX's collectives and lax.ppermute only.
A program may use at most 128 MiB of HBM per device.

```python
import jax
import jax.numpy as jnp
from jax import lax

COLS = 8192
ROWS = 3584
BLOCKS = 4


def levels(stream_key, dims, shards, least, top_value):
    factor_of = 1.0
    for position, parts in shards:
        heights = jax.random.uniform(jax.random.fold_in(jax.random.fold_in(stream_key, 6), position), (parts,), jnp.float32, least / len(shards), top_value / len(shards))
        factor_of = factor_of * jnp.repeat(jnp.exp(heights), dims[position] // parts).reshape((-1,) + (1,) * (len(dims) - 1 - position))
    return factor_of


def noise(stream_key, extent, deviation, most, cuts=(), kind=jnp.bfloat16):
    gain = levels(stream_key, extent, cuts, -0.22, 0.18) if cuts else 1.0
    array = jax.random.normal(stream_key, extent, jnp.float32) * deviation * gain
    return jnp.minimum(jnp.maximum(array, -most), most).astype(kind)


def setup_inputs(seed: int = 0, part: int = 0) -> dict:
    key_of = jax.random.split(jax.random.key(seed), 2)
    part_splits = jax.random.split(jax.random.fold_in(key_of[1], part), 2)
    iterate = noise(part_splits[0], (ROWS, COLS), (4 * COLS) ** -0.5, 0.03125, ((0, 2), (1, 4)))
    return {"iterate": iterate}


coef_linear = 3.4445
coef_cubic = -4.775
coef_quintic = 2.0315

def reference(iterate):
    block_width = COLS // BLOCKS
    col_blocks = iterate.reshape(ROWS, BLOCKS, block_width).transpose(1, 0, 2)

    def add_gram(running, x_block):
        partial_sum = jnp.dot(x_block, x_block.T, preferred_element_type=jnp.float32).astype(jnp.bfloat16)
        partial_sum = lax.optimization_barrier(partial_sum)
        return (running + partial_sum.astype(jnp.float32), None)
    gram_sum, _ = lax.scan(add_gram, jnp.zeros((ROWS, ROWS), jnp.float32), col_blocks)
    gram_sum = gram_sum.astype(jnp.bfloat16)
    square_width = ROWS // BLOCKS
    left_blocks = gram_sum.reshape(ROWS, BLOCKS, square_width).transpose(1, 0, 2)
    right_blocks = gram_sum.reshape(BLOCKS, square_width, ROWS)

    def add_square(running, pair_blocks):
        partial_sum = jnp.dot(pair_blocks[0], pair_blocks[1], preferred_element_type=jnp.float32).astype(jnp.bfloat16)
        partial_sum = lax.optimization_barrier(partial_sum)
        return (running + partial_sum.astype(jnp.float32), None)
    square, _ = lax.scan(add_square, jnp.zeros((ROWS, ROWS), jnp.float32), (left_blocks, right_blocks))
    combo = (coef_cubic * gram_sum.astype(jnp.float32) + coef_quintic * square).astype(jnp.bfloat16)
    product = jnp.dot(combo, iterate, preferred_element_type=jnp.float32)
    scale_factor = 0.2 * jnp.sqrt(jnp.float32(COLS))
    return (scale_factor * (coef_linear * iterate.astype(jnp.float32) + product)).astype(jnp.bfloat16)
```

```python
import functools
import math

import jax
import jax.numpy as jnp
from jax import lax
from jax.experimental import pallas as pl
from jax.experimental.pallas import tpu as pltpu
from jax.sharding import PartitionSpec as P

coef_linear = 3.4445
coef_cubic = -4.775
coef_quintic = 2.0315

bf16 = jnp.bfloat16
f32 = jnp.float32
TILE = 256
LARGE = 48 * 1024 * 1024
SMALL = 28 * 1024 * 1024
TINY = pl.CostEstimate(flops=1024, bytes_accessed=1024, transcendentals=0)


def dot(left_side, right_side, left_dim, right_dim):
    return lax.dot_general(
        left_side, right_side, (((left_dim,), (right_dim,)), ((), ())), preferred_element_type=f32
    )


def shift(size, by):
    return [((i + by) % size, i) for i in range(size)]


def rows_of(array, start, count):
    return lax.dynamic_slice(array, (start, 0), (count, array.shape[1]))


def tie(values, after):
    return lax.optimization_barrier((values, after))[0]


def piece_widths(rows):
    units = rows // TILE
    wide = max(0, (units - 3) // 2)
    return [2 * TILE] * wide + [TILE] * (units - 2 * wide)


def own_widths(rows):
    units = rows // TILE
    widths = []
    while units > 3:
        widths.append(2 * TILE)
        units -= 2
    return widths + [units * TILE]


def strip_body(start, offset, counts, rep_ref, piece_ref, own_ref, *refs):
    above = refs[: len(counts)]
    *outs, held_ref, sems = refs[len(counts) :]
    held, outs = outs[-len(counts) :] if counts else [], outs[: len(outs) - len(counts)]
    parts = len(outs) // 2
    width = held_ref.shape[0]
    height = width // 2
    step = pl.program_id(0)
    first = rep_ref[0] == 0
    copies = [pltpu.make_async_copy(piece_ref.at[pl.ds(offset, width), :], held_ref, sems.at[0])]
    copies += [pltpu.make_async_copy(ref, to, sems.at[1 + i]) for i, (ref, to) in enumerate(zip(above, held))]

    @pl.when(step == 0)
    def _():
        for copy in copies:
            copy.start()
        copies[0].wait()

    def store(part, at, product):
        low, high = product[:, :height], product[:, height:]
        count = product.shape[0]
        outs[part][pl.ds(at, count), :] = jnp.where(first, high, low).astype(bf16)
        outs[parts + part][pl.ds(at, count), :] = jnp.where(first, low, high).astype(bf16)

    if start:
        tile = own_ref.shape[0]
        store(0, pl.multiple_of(step * tile, 64), dot(own_ref[...], held_ref[...], 1, 1))

    @pl.when(step == pl.num_programs(0) - 1)
    def _():
        at = 0 if parts == 2 else start
        for copy, ref in zip(copies[1:], held):
            copy.wait()
            store(1, at, dot(ref[...], held_ref[...], 1, 1))
            at += ref.shape[0]
        store(parts - 1, at, dot(held_ref[...], held_ref[...], 1, 1))


def strip(rep, piece, iterate, above, start, offset, width):
    own, inner = iterate.shape
    height = width // 2
    reach = min(start, own)
    steps = 4 if start else 1
    tile = reach // 4 if start else 64
    counts = [array.shape[0] for array in above]
    heights = [own, start + width - own] if start >= own else [start + width]
    outs = [jax.ShapeDtypeStruct((count, height), bf16) for count in heights] * 2
    any_spec = pl.BlockSpec(memory_space=pl.ANY)
    return pl.pallas_call(
        functools.partial(strip_body, start, offset, counts),
        grid=(steps,),
        in_specs=[pl.BlockSpec(memory_space=pltpu.SMEM), any_spec, pl.BlockSpec((tile, inner), lambda t: (t, 0))]
        + [any_spec] * len(counts),
        out_specs=[pl.BlockSpec(out.shape, lambda t: (0, 0)) for out in outs],
        out_shape=outs,
        scratch_shapes=[pltpu.VMEM((count, inner), bf16) for count in counts]
        + [pltpu.VMEM((width, inner), bf16), pltpu.SemaphoreType.DMA((1 + len(counts),))],
        compiler_params=pltpu.CompilerParams(vmem_limit_bytes=SMALL),
        cost_estimate=TINY,
        name="strip",
    )(rep, piece, iterate, *above)


def put_body(start, parts, rep_ref, *refs):
    mines, others = refs[:parts], refs[parts : 2 * parts]
    gram_ref, strip_ref, turned_ref, sems = refs[-4:]
    reach, width = strip_ref.shape
    height = width // 2
    first = rep_ref[0] == 0
    base = 0
    for mine_ref, other_ref in zip(mines, others):
        for at in range(0, mine_ref.shape[0], TILE):
            here, there = pl.ds(at, TILE), pl.ds(base + at, TILE)
            mine, other = mine_ref[here, :], other_ref[here, :]
            low, high = jnp.where(first, mine, other), jnp.where(first, other, mine)
            strip_ref[there, :height] = low
            strip_ref[there, height:] = high
            if base + at < start:
                turned_ref[:height, there] = low.T
                turned_ref[height:, there] = high.T
        base += mine_ref.shape[0]
    down = pltpu.make_async_copy(strip_ref, gram_ref.at[pl.ds(0, reach), pl.ds(start, width)], sems.at[0])
    down.start()
    if start:
        across = pltpu.make_async_copy(
            turned_ref, gram_ref.at[pl.ds(start, width), pl.ds(0, start)], sems.at[1]
        )
        across.start()
        across.wait()
    down.wait()


def put(rep, gram, rows, start, mines, others):
    height = mines[0].shape[1]
    reach = sum(mine.shape[0] for mine in mines)
    width = 2 * height
    any_spec = pl.BlockSpec(memory_space=pl.ANY)
    first = gram is None
    return pl.pallas_call(
        functools.partial(put_body, start, len(mines)),
        grid=(1,),
        in_specs=[pl.BlockSpec(memory_space=pltpu.SMEM)]
        + [pl.BlockSpec(mine.shape, lambda t: (0, 0)) for mine in mines] * 2
        + ([] if first else [any_spec]),
        out_specs=any_spec,
        out_shape=jax.ShapeDtypeStruct((rows, rows), bf16),
        scratch_shapes=[
            pltpu.VMEM((reach, width), bf16),
            pltpu.VMEM((width, max(start, TILE)), bf16),
            pltpu.SemaphoreType.DMA((2,)),
        ],
        input_output_aliases={} if first else {1 + 2 * len(mines): 0},
        compiler_params=pltpu.CompilerParams(vmem_limit_bytes=SMALL),
        cost_estimate=TINY,
        name="put",
    )(rep, *mines, *others, *([] if first else [gram]))


def product_body(other, scale, count, rep_ref, combo_ref, linear_ref, *refs):
    out_ref = refs[-1]
    total, at = scale * coef_linear * linear_ref[...].astype(f32), 0
    summed = None
    for ref in refs[:count]:
        rows = ref.shape[0]
        product = dot(combo_ref[:, at : at + rows], ref[...], 1, 0)
        summed = product if summed is None else summed + product
        at += rows
    out_ref[...] = (total + scale * summed).astype(bf16)


def product(rep, combo, panels, iterate, before, scale):
    share, rows = combo.shape
    own, inner = iterate.shape
    other = before is not None
    tile = TILE
    place = (lambda n, rep: (1 - rep[0], n)) if other else (lambda n, rep: (rep[0], n))
    return pl.pallas_call(
        functools.partial(product_body, other, scale, len(panels)),
        grid_spec=pltpu.PrefetchScalarGridSpec(
            num_scalar_prefetch=1,
            grid=(inner // tile,),
            in_specs=[
                pl.BlockSpec((share, rows), lambda n, rep: (0, 0)),
                pl.BlockSpec((share, tile), place),
            ]
            + [pl.BlockSpec((panel.shape[0], tile), lambda n, rep: (0, n)) for panel in panels]
            + [pl.BlockSpec(memory_space=pl.ANY)] * other,
            out_specs=pl.BlockSpec((share, tile), place),
        ),
        out_shape=jax.ShapeDtypeStruct((own, inner), bf16),
        input_output_aliases={3 + len(panels): 0} if other else {},
        compiler_params=pltpu.CompilerParams(vmem_limit_bytes=LARGE),
        cost_estimate=pl.CostEstimate(flops=2 * share * rows * inner, bytes_accessed=2 * rows * inner, transcendentals=0),
        name="product",
    )(rep, combo, iterate, *panels, *([before] if other else []))


def add(left_side, right_side):
    return (left_side.astype(f32) + right_side.astype(f32)).astype(bf16)


def adds(arrays):
    half = len(arrays) // 2
    return [add(*pair) for pair in zip(arrays[:half], arrays[half:])]


def local(iterate, sizes):
    own, inner = iterate.shape
    rows = own * sizes["row"]
    cols = inner * sizes["rep"] * sizes["col"]
    share = own // 2
    swap = [(0, 1), (1, 0)]
    rep = lax.axis_index("rep")
    rep_ref = rep.astype(jnp.int32).reshape(1)
    mine_at = rep * share

    widths = piece_widths(own)
    pieces = []
    at = 0
    for width in widths:
        source = iterate[at : at + width]
        if len(pieces) >= 2:
            source = tie(source, pieces[-2])
        pieces.append(lax.ppermute(source, "row", swap))
        at += width

    state = {"last": rep_ref}

    def step(function, *args):
        out = function(*tie(args, state["last"]))
        state["last"] = out[-1] if isinstance(out, (tuple, list)) else out
        return out

    class Strip:
        def __init__(self, start, width):
            self.start, self.width = start, width

        def multiply(self, piece, above, offset=0):
            out = step(
                lambda piece, *above: strip(rep_ref, piece, iterate, above, self.start, offset, self.width),
                piece,
                *above,
            )
            half = len(out) // 2
            self.kept = out[half:]
            self.taken = [lax.ppermute(sent, "rep", swap) for sent in out[:half]]

        def chip(self):
            self.part = step(lambda *a: adds(a), *self.kept, *self.taken)
            self.across = [lax.ppermute(part, "col", swap) for part in self.part]

        def total(self):
            self.mine = step(lambda *a: adds(a), *self.part, *self.across)
            self.other = [lax.ppermute(mine, "rep", swap) for mine in self.mine]

        def put(self):
            before = () if state.get("gram") is None else (state["gram"],)
            parts = len(self.mine)
            state["gram"] = step(
                lambda *a: put(
                    rep_ref, a[2 * parts] if before else None, rows, self.start, a[:parts], a[parts : 2 * parts]
                ),
                *self.mine,
                *self.other,
                *before,
            )

    owns, start = [], 0
    for width in own_widths(own):
        item = Strip(start, width)
        item.multiply(iterate, [], start)
        if owns:
            owns[-1].chip()
        owns.append(item)
        start += width
    owns[-1].chip()
    others = []
    for width in widths:
        others.append(Strip(start, width))
        start += width

    def arrive(index, before=()):
        others[index].multiply(pieces[index], pieces[:index])
        for item in before:
            item.total()
        others[index].chip()
        for item in before:
            item.put()

    blocks = []

    def grow(edge, last):
        def widen(gram, *squares):
            near = lax.dynamic_slice(gram, (mine_at, edge), (share, last - edge))
            out = []
            for (low, high), square in zip(blocks, squares):
                out.append(square + dot(near, gram[edge:last, low:high], 1, 0))
            fresh = lax.dynamic_slice(gram, (mine_at, 0), (share, last))
            out.append(dot(fresh, gram[:last, edge:last], 1, 0))
            return out

        state["squares"] = step(widen, state["gram"], *state.get("squares", []))
        blocks.append((edge, last))

    owns[0].total()
    owns[0].put()
    arrive(0, [owns[1]])
    arrive(1, [owns[2], others[0]])
    grow(0, others[1].start)
    arrive(2, [others[1]])
    arrive(3, [others[2]])
    arrive(4, [others[3]])
    grow(others[1].start, others[3].start)
    others[4].total()
    others[4].put()
    edge = others[3].start

    def finish(gram, *squares):
        mine = lax.dynamic_slice(gram, (mine_at, 0), (share, rows))
        near = mine[:, edge:]
        parts = [
            coef_cubic * mine[:, low:high].astype(f32) + coef_quintic * (square + dot(near, gram[edge:, low:high], 1, 0))
            for (low, high), square in zip(blocks, squares)
        ]
        parts.append(coef_cubic * near.astype(f32) + coef_quintic * dot(mine, gram[:, edge:], 1, 0))
        return jnp.concatenate([part.astype(bf16) for part in parts], axis=1)

    combo = step(finish, state["gram"], *state["squares"])
    scale_factor = 0.2 * math.sqrt(cols)
    theirs = lax.ppermute(combo, "rep", swap)
    result = product(rep_ref, combo, [iterate, *pieces], iterate, None, scale_factor)
    return product(rep_ref, theirs, [iterate, *pieces], iterate, result, scale_factor)


def general(iterate, sizes):
    row_size, rep_size = sizes["row"], sizes["rep"]
    own, inner = iterate.shape
    rows = own * row_size
    cols = inner * rep_size * sizes["col"]
    panel = jnp.concatenate(
        [iterate] + [lax.ppermute(iterate, "row", shift(row_size, by)) for by in range(1, row_size)]
    )
    gram = lax.psum(dot(panel, panel, 1, 1), ("rep", "col")).astype(bf16)
    share = own // rep_size
    mine = lax.dynamic_slice(gram, (0, lax.axis_index("rep") * share), (rows, share))
    combo = (coef_cubic * mine.astype(f32) + coef_quintic * dot(gram, mine, 1, 0)).astype(bf16)
    combo = lax.all_gather(combo, "rep", axis=1, tiled=True)
    scale_factor = 0.2 * jnp.sqrt(f32(cols))
    return (scale_factor * (coef_linear * iterate.astype(f32) + dot(combo, panel, 0, 0))).astype(bf16)


def solution(mesh):
    spec = P(("layer", "row"), ("rep", "col"))
    sizes = dict(mesh.shape)

    def body(iterate):
        pairs = all(sizes[axis] == 2 for axis in ("row", "rep", "col"))
        fits = iterate.shape[0] % TILE == 0 and len(piece_widths(iterate.shape[0])) == 5
        return (local if pairs and fits else general)(iterate, sizes)

    return jax.shard_map(body, mesh=mesh, in_specs=(spec,), out_specs=spec, check_vma=False)
```

```python
import functools
import math

import jax
import jax.numpy as jnp
from jax import lax
from jax.experimental import pallas as pl
from jax.experimental.pallas import tpu as pltpu
from jax.sharding import PartitionSpec as P

coef_linear = 3.4445
coef_cubic = -4.775
coef_quintic = 2.0315

bf16 = jnp.bfloat16
f32 = jnp.float32
TILE = 256
LARGE = 48 * 1024 * 1024
SMALL = 28 * 1024 * 1024
SCALE = 0.36e9


def cost(microseconds):
    return pl.CostEstimate(flops=int(microseconds * SCALE), bytes_accessed=1024, transcendentals=0)


def dot(left_side, right_side, left_dim, right_dim):
    return lax.dot_general(
        left_side, right_side, (((left_dim,), (right_dim,)), ((), ())), preferred_element_type=f32
    )


def shift(size, by):
    return [((i + by) % size, i) for i in range(size)]


def rows_of(array, start, count):
    return lax.dynamic_slice(array, (start, 0), (count, array.shape[1]))


def tie(values, after):
    return lax.optimization_barrier((values, after))[0]


def piece_widths(rows):
    units = rows // TILE
    widths = [2 * TILE] * (units // 2)
    return widths[:1] + [TILE] * (units % 2) + widths[1:]


def own_widths(rows):
    units = rows // TILE
    widths = []
    while units > 3:
        widths.append(2 * TILE)
        units -= 2
    return widths + [units * TILE]


def strip_body(start, offset, counts, heights, only, rep_ref, piece_ref, own_ref, *refs):
    above = refs[: len(counts)]
    refs = refs[len(counts) :]
    sents, kept_ref = refs[: len(heights)], refs[len(heights)]
    held, (held_ref, sems) = refs[len(heights) + 1 : -2], refs[-2:]
    width = held_ref.shape[0]
    height = width // 2
    step = pl.program_id(0)
    first = rep_ref[0] == 0
    copies = [pltpu.make_async_copy(piece_ref.at[pl.ds(offset, width), :], held_ref, sems.at[0])]
    copies += [pltpu.make_async_copy(ref, to, sems.at[1 + i]) for i, (ref, to) in enumerate(zip(above, held))]

    @pl.when(step == 0)
    def _():
        for copy in copies:
            copy.start()
        copies[0].wait()

    def store(index, product):
        low, high = product[:, :height], product[:, height:]
        at = sum(heights[:index])
        sents[index][...] = jnp.where(first, high, low).astype(bf16)
        kept_ref[at : at + heights[index], :] = jnp.where(first, low, high).astype(bf16)

    steps = 4 if start else 0
    for index in range(steps):

        @pl.when(step == index)
        def _(index=index):
            store(index, dot(own_ref[...], held_ref[...], 1, 1))

    if not only:

        @pl.when(step == pl.num_programs(0) - 1)
        def _():
            for index, (copy, ref) in enumerate(zip(copies[1:], held)):
                copy.wait()
                store(steps + index, dot(ref[...], held_ref[...], 1, 1))
            store(len(heights) - 1, dot(held_ref[...], held_ref[...], 1, 1))


def strip(rep, piece, iterate, above, start, offset, width, only=False):
    own, inner = iterate.shape
    height = width // 2
    reach = min(start, own)
    tile = reach // 4 if start else 64
    above = [] if only else list(above)
    counts = [array.shape[0] for array in above]
    heights = [tile] * (4 if start else 0) + ([] if only else counts + [width])
    outs = [jax.ShapeDtypeStruct((count, height), bf16) for count in heights + [sum(heights)]]
    any_spec = pl.BlockSpec(memory_space=pl.ANY)
    return pl.pallas_call(
        functools.partial(strip_body, start, offset, counts, heights, only),
        grid=(4 if start else 1,),
        in_specs=[pl.BlockSpec(memory_space=pltpu.SMEM), any_spec, pl.BlockSpec((tile, inner), lambda t: (t, 0))]
        + [any_spec] * len(counts),
        out_specs=[pl.BlockSpec(out.shape, lambda t: (0, 0)) for out in outs],
        out_shape=outs,
        scratch_shapes=[pltpu.VMEM((count, inner), bf16) for count in counts]
        + [pltpu.VMEM((width, inner), bf16), pltpu.SemaphoreType.DMA((1 + len(counts),))],
        compiler_params=pltpu.CompilerParams(vmem_limit_bytes=SMALL),
        cost_estimate=cost(1 + 4 * height * sum(heights) * inner / 0.8e9),
        name="strip",
    )(rep, piece, iterate, *above)


def put_body(start, parts, rep_ref, *refs):
    mines, others = refs[: parts[0]], refs[parts[0] : sum(parts)]
    gram_ref, strip_ref, turned_ref, sems = refs[-4:]
    reach, width = strip_ref.shape
    height = width // 2
    first = rep_ref[0] == 0

    def rows_at(arrays, at):
        for array in arrays:
            if at < array.shape[0]:
                return array[pl.ds(at, TILE), :]
            at -= array.shape[0]

    for at in range(0, reach, TILE):
        there = pl.ds(at, TILE)
        mine, other = rows_at(mines, at), rows_at(others, at)
        low, high = jnp.where(first, mine, other), jnp.where(first, other, mine)
        strip_ref[there, :height] = low
        strip_ref[there, height:] = high
        if at < start:
            turned_ref[:height, there] = low.T
            turned_ref[height:, there] = high.T
    down = pltpu.make_async_copy(strip_ref, gram_ref.at[pl.ds(0, reach), pl.ds(start, width)], sems.at[0])
    down.start()
    if start:
        across = pltpu.make_async_copy(
            turned_ref, gram_ref.at[pl.ds(start, width), pl.ds(0, start)], sems.at[1]
        )
        across.start()
        across.wait()
    down.wait()


def put(rep, gram, rows, start, mines, others):
    height = mines[0].shape[1]
    reach = sum(mine.shape[0] for mine in mines)
    width = 2 * height
    any_spec = pl.BlockSpec(memory_space=pl.ANY)
    first = gram is None
    arrays = [*mines, *others]
    return pl.pallas_call(
        functools.partial(put_body, start, (len(mines), len(others))),
        grid=(1,),
        in_specs=[pl.BlockSpec(memory_space=pltpu.SMEM)]
        + [pl.BlockSpec(array.shape, lambda t: (0, 0)) for array in arrays]
        + ([] if first else [any_spec]),
        out_specs=any_spec,
        out_shape=jax.ShapeDtypeStruct((rows, rows), bf16),
        scratch_shapes=[
            pltpu.VMEM((reach, width), bf16),
            pltpu.VMEM((width, max(start, TILE)), bf16),
            pltpu.SemaphoreType.DMA((2,)),
        ],
        input_output_aliases={} if first else {1 + len(arrays): 0},
        compiler_params=pltpu.CompilerParams(vmem_limit_bytes=LARGE),
        cost_estimate=cost(3),
        name="put",
    )(rep, *arrays, *([] if first else [gram]))


def square_body(low, column, base, last, rep_ref, near_ref, gram_ref, *refs):
    if base:
        base_ref, *refs = refs
    *_, out_ref, left_ref, right_ref, sems = refs
    share, inner = left_ref.shape
    step = pl.program_id(0)
    slot = lax.rem(step, 2)

    def fetch(step, slot):
        at = pl.multiple_of(column + step * TILE, TILE)
        return pltpu.make_async_copy(
            gram_ref.at[pl.ds(low, inner), pl.ds(at, TILE)], right_ref.at[slot], sems.at[1 + slot]
        )

    rows_at = pl.multiple_of(rep_ref[0] * share, 128)
    left = pltpu.make_async_copy(gram_ref.at[pl.ds(rows_at, share), pl.ds(low, inner)], left_ref, sems.at[0])

    @pl.when(step == 0)
    def _():
        left.start()
        fetch(step, slot).start()
        left.wait()

    @pl.when(step + 1 < pl.num_programs(0))
    def _():
        fetch(step + 1, 1 - slot).start()

    fetch(step, slot).wait()
    total = dot(left_ref[...], right_ref[slot], 1, 0)
    if base:
        total = total + base_ref[0]
    if last:
        out_ref[...] = (coef_cubic * near_ref[...].astype(f32) + coef_quintic * total).astype(bf16)
    else:
        out_ref[0] = total


def square(rep, gram, into, low, high, left, right, base, last):
    rows = gram.shape[0]
    share = rows // 4
    block = left // TILE
    any_spec = pl.BlockSpec(memory_space=pl.ANY)
    tiles = pl.BlockSpec((1, share, TILE), lambda n, rep: (block + n, 0, 0))
    columns = pl.BlockSpec((share, TILE), lambda n, rep: (0, block + n)) if last else tiles
    shape = (share, rows) if last else (rows // TILE, share, TILE)
    operands = [gram, gram]
    specs = [pl.BlockSpec((share, TILE), lambda n, rep: (rep[0], block + n)), any_spec]
    alias = {}
    if base is not None:
        operands.append(base)
        specs.append(tiles)
        if base is into:
            alias = {len(operands): 0}
    if into is not None and into is not base:
        operands.append(into)
        specs.append(any_spec)
        alias = {len(operands): 0}
    return pl.pallas_call(
        functools.partial(square_body, low, left, base is not None, last),
        grid_spec=pltpu.PrefetchScalarGridSpec(
            num_scalar_prefetch=1,
            grid=((right - left) // TILE,),
            in_specs=specs,
            out_specs=columns,
            scratch_shapes=[
                pltpu.VMEM((share, high - low), bf16),
                pltpu.VMEM((2, high - low, TILE), bf16),
                pltpu.SemaphoreType.DMA((3,)),
            ],
        ),
        out_shape=jax.ShapeDtypeStruct(shape, bf16 if last else f32),
        input_output_aliases=alias,
        compiler_params=pltpu.CompilerParams(vmem_limit_bytes=LARGE),
        cost_estimate=cost(3 + 2 * share * (high - low) * (right - left) / 0.6e9),
        name="square",
    )(rep, *operands)


def product_body(other, scale, count, rep_ref, combo_ref, linear_ref, *refs):
    out_ref = refs[-1]
    total, at = scale * coef_linear * linear_ref[...].astype(f32), 0
    summed = None
    for ref in refs[:count]:
        rows = ref.shape[0]
        product = dot(combo_ref[:, at : at + rows], ref[...], 1, 0)
        summed = product if summed is None else summed + product
        at += rows
    out_ref[...] = (total + scale * summed).astype(bf16)


def product(rep, combo, panels, iterate, before, scale):
    share, rows = combo.shape
    own, inner = iterate.shape
    other = before is not None
    tile = TILE
    place = (lambda n, rep: (1 - rep[0], n)) if other else (lambda n, rep: (rep[0], n))
    return pl.pallas_call(
        functools.partial(product_body, other, scale, len(panels)),
        grid_spec=pltpu.PrefetchScalarGridSpec(
            num_scalar_prefetch=1,
            grid=(inner // tile,),
            in_specs=[
                pl.BlockSpec((share, rows), lambda n, rep: (0, 0)),
                pl.BlockSpec((share, tile), place),
            ]
            + [pl.BlockSpec((panel.shape[0], tile), lambda n, rep: (0, n)) for panel in panels]
            + [pl.BlockSpec(memory_space=pl.ANY)] * other,
            out_specs=pl.BlockSpec((share, tile), place),
        ),
        out_shape=jax.ShapeDtypeStruct((own, inner), bf16),
        input_output_aliases={3 + len(panels): 0} if other else {},
        compiler_params=pltpu.CompilerParams(vmem_limit_bytes=LARGE),
        cost_estimate=pl.CostEstimate(flops=2 * share * rows * inner // 3, bytes_accessed=1024, transcendentals=0),
        name="product",
    )(rep, combo, iterate, *panels, *([before] if other else []))


def add_body(parts, array_ref, *refs):
    seconds, whole_ref, outs = refs[:parts], refs[parts], refs[parts + 1 :]
    at = 0
    for ref in seconds:
        rows = pl.ds(at, ref.shape[0])
        whole_ref[rows, :] = (array_ref[rows, :].astype(f32) + ref[...].astype(f32)).astype(bf16)
        at += ref.shape[0]
    at = 0
    for ref in outs:
        ref[...] = whole_ref[pl.ds(at, ref.shape[0]), :]
        at += ref.shape[0]


def add(array, *seconds, split=False):
    shapes = [array.shape] + ([chunk.shape for chunk in jax.eval_shape(chunks, array)] if split else [])
    full = lambda shape: pl.BlockSpec(shape, lambda t: (0, 0))
    return pl.pallas_call(
        functools.partial(add_body, len(seconds)),
        grid=(1,),
        in_specs=[full(x.shape) for x in (array, *seconds)],
        out_specs=[full(shape) for shape in shapes],
        out_shape=[jax.ShapeDtypeStruct(shape, bf16) for shape in shapes],
        compiler_params=pltpu.CompilerParams(vmem_limit_bytes=SMALL),
        cost_estimate=cost(1.5),
        name="add",
    )(array, *seconds)


def chunks(array):
    rows, columns = array.shape
    size = max(TILE, 128 * 1024 // columns // TILE * TILE)
    return [array[at : min(at + size, rows)] for at in range(0, rows, size)]


def local(iterate, sizes):
    own, inner = iterate.shape
    rows = own * sizes["row"]
    cols = inner * sizes["rep"] * sizes["col"]
    share = own // 2
    swap = [(0, 1), (1, 0)]
    rep = lax.axis_index("rep")
    rep_ref = rep.astype(jnp.int32).reshape(1)
    mine_at = rep * share

    widths = piece_widths(own)
    pieces = []
    at = 0
    for width in widths:
        source = iterate[at : at + width]
        if len(pieces) >= 2:
            source = tie(source, pieces[-2])
        pieces.append(lax.ppermute(source, "row", swap))
        at += width

    state = {"last": rep_ref}

    def step(function, *args):
        out = function(*tie(args, state["last"]))
        state["last"] = out[-1] if isinstance(out, (tuple, list)) else out
        return out

    class Strip:
        def __init__(self, start, width):
            self.start, self.width = start, width

        def multiply(self, piece, above, offset=0, only=False):
            *sent, self.kept = step(
                lambda piece, *above: strip(rep_ref, piece, iterate, above, self.start, offset, self.width, only),
                piece,
                *above,
            )
            self.taken = [lax.ppermute(chunk, "rep", swap) for chunk in sent]

        def chip(self):
            self.part = step(lambda *a: add(*a)[0], self.kept, *self.taken)
            self.across = lax.ppermute(self.part, "col", swap)

        def total(self, lower=()):
            mine, *self.other = step(
                lambda a, b: add(a, b, split=True), self.part, self.across
            )
            self.mine = [mine, *lower]
            self.other = [lax.ppermute(chunk, "rep", swap) for chunk in self.other]

        def put(self, lower=()):
            before = () if state.get("gram") is None else (state["gram"],)
            parts = len(self.mine)
            arrays = [*self.mine, *self.other, *lower]
            state["gram"] = step(
                lambda *a: put(
                    rep_ref,
                    a[-1] if before else None,
                    rows,
                    self.start,
                    a[:parts],
                    a[parts : len(arrays)],
                ),
                *arrays,
                *before,
            )

    owns, start = [], 0
    for width in own_widths(own):
        item = Strip(start, width)
        item.multiply(iterate, [], start)
        owns.append(item)
        start += width
    for item in owns:
        item.chip()
    others = []
    for width in widths:
        others.append(Strip(start, width))
        start += width

    def arrive(index, before=(), only=False):
        others[index].multiply(pieces[index], pieces[:index], only=only)
        for item in before:
            item.total()
        others[index].chip()
        for item in before:
            item.put()

    def grow(edge, last):
        def widen(gram, *sums):
            sums = sums[0] if sums else None
            if edge:
                sums = square(rep_ref, gram, sums, edge, last, 0, edge, sums, False)
            return square(rep_ref, gram, sums, 0, last, edge, last, None, False)

        state["sums"] = step(widen, state["gram"], *([state["sums"]] if edge else []))

    def finish(item):
        item.total()
        item.put()

    arrive(0)
    arrive(1, owns)
    width = widths[-1]
    lower = lax.dynamic_slice(state["gram"], (0, own - width + rep * (width // 2)), (own, width // 2))
    lower = lax.ppermute(tie(lower, pieces[-1]), "row", swap)
    grow(0, own)
    finish(others[0])
    finish(others[1])
    arrive(2)
    grow(own, others[2].start)
    arrive(3, [others[2]], only=True)
    grow(others[2].start, others[3].start)
    last = others[3]
    lower, *lows = step(lambda a: [a, *chunks(a)], lower)
    lows = [lax.ppermute(chunk, "rep", swap) for chunk in lows]
    last.total([lower])
    last.put(lows)
    edge = last.start

    def close(gram, sums):
        combo = square(rep_ref, gram, None, edge, rows, 0, edge, sums, True)
        return square(rep_ref, gram, combo, 0, rows, edge, rows, None, True)

    combo = step(close, state["gram"], state["sums"])
    scale_factor = 0.2 * math.sqrt(cols)
    theirs = lax.ppermute(combo, "rep", swap)
    result = product(rep_ref, combo, [iterate, *pieces], iterate, None, scale_factor)
    return product(rep_ref, theirs, [iterate, *pieces], iterate, result, scale_factor)


def general(iterate, sizes):
    row_size, rep_size = sizes["row"], sizes["rep"]
    own, inner = iterate.shape
    rows = own * row_size
    cols = inner * rep_size * sizes["col"]
    panel = jnp.concatenate(
        [iterate] + [lax.ppermute(iterate, "row", shift(row_size, by)) for by in range(1, row_size)]
    )
    gram = lax.psum(dot(panel, panel, 1, 1), ("rep", "col")).astype(bf16)
    share = own // rep_size
    mine = lax.dynamic_slice(gram, (0, lax.axis_index("rep") * share), (rows, share))
    combo = (coef_cubic * mine.astype(f32) + coef_quintic * dot(gram, mine, 1, 0)).astype(bf16)
    combo = lax.all_gather(combo, "rep", axis=1, tiled=True)
    scale_factor = 0.2 * jnp.sqrt(f32(cols))
    return (scale_factor * (coef_linear * iterate.astype(f32) + dot(combo, panel, 0, 0))).astype(bf16)


def solution(mesh):
    spec = P(("layer", "row"), ("rep", "col"))
    sizes = dict(mesh.shape)

    def body(iterate):
        pairs = all(sizes[axis] == 2 for axis in ("row", "rep", "col"))
        fits = iterate.shape[0] % TILE == 0 and len(piece_widths(iterate.shape[0])) == 4
        return (local if pairs and fits else general)(iterate, sizes)

    return jax.shard_map(body, mesh=mesh, in_specs=(spec,), out_specs=spec, check_vma=False)
```

```python
import functools
import math

import jax
import jax.numpy as jnp
from jax import lax
from jax.experimental import pallas as pl
from jax.experimental.pallas import tpu as pltpu
from jax.sharding import PartitionSpec as P

coef_linear = 3.4445
coef_cubic = -4.775
coef_quintic = 2.0315

bf16 = jnp.bfloat16
f32 = jnp.float32
TILE = 256
LARGE = 48 * 1024 * 1024
SMALL = 28 * 1024 * 1024
SCALE = 0.06e9


def cost(microseconds):
    return pl.CostEstimate(flops=int(microseconds * SCALE), bytes_accessed=1024, transcendentals=0)


def dot(left_side, right_side, left_dim, right_dim):
    return lax.dot_general(
        left_side, right_side, (((left_dim,), (right_dim,)), ((), ())), preferred_element_type=f32
    )


def shift(size, by):
    return [((i + by) % size, i) for i in range(size)]


def rows_of(array, start, count):
    return lax.dynamic_slice(array, (start, 0), (count, array.shape[1]))


def tie(values, after):
    return lax.optimization_barrier((values, after))[0]


def piece_widths(rows):
    units = rows // TILE
    widths = [2 * TILE] * (units // 2)
    return widths[:1] + [TILE] * (units % 2) + widths[1:]


def own_widths(rows):
    units = rows // TILE
    widths = []
    while units > 3:
        widths.append(2 * TILE)
        units -= 2
    return widths + [units * TILE]


def strip_body(start, offset, counts, heights, only, rep_ref, piece_ref, own_ref, *refs):
    above = refs[: len(counts)]
    refs = refs[len(counts) :]
    sents, kept_ref = refs[: len(heights)], refs[len(heights)]
    held, (held_ref, sems) = refs[len(heights) + 1 : -2], refs[-2:]
    width = held_ref.shape[0]
    height = width // 2
    step = pl.program_id(0)
    first = rep_ref[0] == 0
    copies = [pltpu.make_async_copy(piece_ref.at[pl.ds(offset, width), :], held_ref, sems.at[0])]
    copies += [pltpu.make_async_copy(ref, to, sems.at[1 + i]) for i, (ref, to) in enumerate(zip(above, held))]

    @pl.when(step == 0)
    def _():
        for copy in copies:
            copy.start()
        copies[0].wait()

    def store(index, product):
        low, high = product[:, :height], product[:, height:]
        at = sum(heights[:index])
        sents[index][...] = jnp.where(first, high, low).astype(bf16)
        kept_ref[at : at + heights[index], :] = jnp.where(first, low, high).astype(bf16)

    steps = 4 if start else 0
    for index in range(steps):

        @pl.when(step == index)
        def _(index=index):
            store(index, dot(own_ref[...], held_ref[...], 1, 1))

    if not only:

        @pl.when(step == pl.num_programs(0) - 1)
        def _():
            for index, (copy, ref) in enumerate(zip(copies[1:], held)):
                copy.wait()
                store(steps + index, dot(ref[...], held_ref[...], 1, 1))
            store(len(heights) - 1, dot(held_ref[...], held_ref[...], 1, 1))


def strip(rep, piece, iterate, above, start, offset, width, only=False):
    own, inner = iterate.shape
    height = width // 2
    reach = min(start, own)
    tile = reach // 4 if start else 64
    above = [] if only else list(above)
    counts = [array.shape[0] for array in above]
    heights = [tile] * (4 if start else 0) + ([] if only else counts + [width])
    outs = [jax.ShapeDtypeStruct((count, height), bf16) for count in heights + [sum(heights)]]
    any_spec = pl.BlockSpec(memory_space=pl.ANY)
    return pl.pallas_call(
        functools.partial(strip_body, start, offset, counts, heights, only),
        grid=(4 if start else 1,),
        in_specs=[pl.BlockSpec(memory_space=pltpu.SMEM), any_spec, pl.BlockSpec((tile, inner), lambda t: (t, 0))]
        + [any_spec] * len(counts),
        out_specs=[pl.BlockSpec(out.shape, lambda t: (0, 0)) for out in outs],
        out_shape=outs,
        scratch_shapes=[pltpu.VMEM((count, inner), bf16) for count in counts]
        + [pltpu.VMEM((width, inner), bf16), pltpu.SemaphoreType.DMA((1 + len(counts),))],
        compiler_params=pltpu.CompilerParams(vmem_limit_bytes=SMALL),
        cost_estimate=cost(1 + 4 * height * sum(heights) * inner / 0.8e9),
        name="strip",
    )(rep, piece, iterate, *above)


def put_body(start, parts, rep_ref, *refs):
    mines, others = refs[: parts[0]], refs[parts[0] : sum(parts)]
    gram_ref, strip_ref, turned_ref, sems = refs[-4:]
    reach, width = strip_ref.shape
    height = width // 2
    first = rep_ref[0] == 0

    def rows_at(arrays, at):
        for array in arrays:
            if at < array.shape[0]:
                return array[pl.ds(at, TILE), :]
            at -= array.shape[0]

    for at in range(0, reach, TILE):
        there = pl.ds(at, TILE)
        mine, other = rows_at(mines, at), rows_at(others, at)
        low, high = jnp.where(first, mine, other), jnp.where(first, other, mine)
        strip_ref[there, :height] = low
        strip_ref[there, height:] = high
        if at < start:
            turned_ref[:height, there] = low.T
            turned_ref[height:, there] = high.T
    down = pltpu.make_async_copy(strip_ref, gram_ref.at[pl.ds(0, reach), pl.ds(start, width)], sems.at[0])
    down.start()
    if start:
        across = pltpu.make_async_copy(
            turned_ref, gram_ref.at[pl.ds(start, width), pl.ds(0, start)], sems.at[1]
        )
        across.start()
        across.wait()
    down.wait()


def put(rep, gram, rows, start, mines, others):
    height = mines[0].shape[1]
    reach = sum(mine.shape[0] for mine in mines)
    width = 2 * height
    any_spec = pl.BlockSpec(memory_space=pl.ANY)
    first = gram is None
    arrays = [*mines, *others]
    return pl.pallas_call(
        functools.partial(put_body, start, (len(mines), len(others))),
        grid=(1,),
        in_specs=[pl.BlockSpec(memory_space=pltpu.SMEM)]
        + [pl.BlockSpec(array.shape, lambda t: (0, 0)) for array in arrays]
        + ([] if first else [any_spec]),
        out_specs=any_spec,
        out_shape=jax.ShapeDtypeStruct((rows, rows), bf16),
        scratch_shapes=[
            pltpu.VMEM((reach, width), bf16),
            pltpu.VMEM((width, max(start, TILE)), bf16),
            pltpu.SemaphoreType.DMA((2,)),
        ],
        input_output_aliases={} if first else {1 + len(arrays): 0},
        compiler_params=pltpu.CompilerParams(vmem_limit_bytes=LARGE),
        cost_estimate=cost(3),
        name="put",
    )(rep, *arrays, *([] if first else [gram]))


def square_body(edge, last, tile, rep_ref, gram_ref, *refs):
    refs = list(refs)
    near_ref = refs.pop(0) if last else None
    base_ref = refs.pop(0) if edge else None
    out_ref, left_ref, thin_ref, tall_ref, sems = refs
    share, reach = left_ref.shape
    old = edge // tile
    step = pl.program_id(0)
    slot = lax.rem(step, 2)
    rows_at = pl.multiple_of(rep_ref[0] * share, 128)

    def left(low, high, sem):
        return pltpu.make_async_copy(
            gram_ref.at[pl.ds(rows_at, share), pl.ds(low, high - low)], left_ref.at[:, pl.ds(low, high - low)], sem
        )

    def thin(step, slot):
        at = pl.ds(pl.multiple_of(step * tile, tile), tile)
        return pltpu.make_async_copy(
            gram_ref.at[pl.ds(edge, reach - edge), at], thin_ref.at[slot], sems.at[2 + slot]
        )

    def tall(step, slot):
        at = pl.ds(pl.multiple_of(step * tile, tile), tile)
        return pltpu.make_async_copy(gram_ref.at[pl.ds(0, reach), at], tall_ref.at[slot], sems.at[4 + slot])

    def start(step, slot):
        if edge:

            @pl.when(step < old)
            def _():
                thin(step, slot).start()

        @pl.when((step >= old) & (step < reach // tile))
        def _():
            tall(step, slot).start()

    @pl.when(step == 0)
    def _():
        left(edge, reach, sems.at[0]).start()
        start(step, slot)
        if edge:
            left(0, edge, sems.at[1]).start()
        left(edge, reach, sems.at[0]).wait()

    start(step + 1, 1 - slot)

    def store(total):
        if last:
            out_ref[...] = (coef_cubic * near_ref[...].astype(f32) + coef_quintic * total).astype(bf16)
        else:
            for i in range(tile // TILE):
                out_ref[i] = total[:, i * TILE : (i + 1) * TILE].astype(bf16)

    if edge:

        @pl.when(step < old)
        def _():
            thin(step, slot).wait()
            base = jnp.concatenate([base_ref[i] for i in range(tile // TILE)], axis=1)
            store(base.astype(f32) + dot(left_ref[:, edge:], thin_ref[slot], 1, 0))

        @pl.when(step == old)
        def _():
            left(0, edge, sems.at[1]).wait()

    @pl.when(step >= old)
    def _():
        tall(step, slot).wait()
        store(dot(left_ref[...], tall_ref[slot], 1, 0))


def square(rep, gram, sums, edge, reach, last):
    rows = gram.shape[0]
    share = rows // 4
    wide = 2 * TILE
    tile = TILE if edge % wide or reach % wide else wide
    old = edge // tile
    any_spec = pl.BlockSpec(memory_space=pl.ANY)
    operands, specs = [gram], [any_spec]
    if last:
        operands.append(gram)
        specs.append(pl.BlockSpec((share, tile), lambda n, rep: (rep[0], n)))
    if edge:
        operands.append(sums)
        specs.append(pl.BlockSpec((tile // TILE, share, TILE), lambda n, rep: (jnp.minimum(n, old - 1), 0, 0)))
    if last:
        out, out_spec = (share, rows), pl.BlockSpec((share, tile), lambda n, rep: (0, n))
    else:
        out, out_spec = (rows // TILE, share, TILE), pl.BlockSpec((tile // TILE, share, TILE), lambda n, rep: (n, 0, 0))
    return pl.pallas_call(
        functools.partial(square_body, edge, last, tile),
        grid_spec=pltpu.PrefetchScalarGridSpec(
            num_scalar_prefetch=1,
            grid=(reach // tile,),
            in_specs=specs,
            out_specs=out_spec,
            scratch_shapes=[
                pltpu.VMEM((share, reach), bf16),
                pltpu.VMEM((2, reach - edge if edge else TILE, tile), bf16),
                pltpu.VMEM((2, reach, tile), bf16),
                pltpu.SemaphoreType.DMA((6,)),
            ],
        ),
        out_shape=jax.ShapeDtypeStruct(out, bf16),
        compiler_params=pltpu.CompilerParams(vmem_limit_bytes=LARGE),
        cost_estimate=cost(8 + 5 * share * (edge * (reach - edge) + (reach - edge) * reach) / 0.6e9),
        name="square",
    )(rep, *operands)


def product_body(other, scale, count, rep_ref, combo_ref, linear_ref, *refs):
    out_ref = refs[-1]
    total, at = scale * coef_linear * linear_ref[...].astype(f32), 0
    summed = None
    for ref in refs[:count]:
        rows = ref.shape[0]
        product = dot(combo_ref[:, at : at + rows], ref[...], 1, 0)
        summed = product if summed is None else summed + product
        at += rows
    out_ref[...] = (total + scale * summed).astype(bf16)


def product(rep, combo, panels, iterate, before, scale):
    share, rows = combo.shape
    own, inner = iterate.shape
    other = before is not None
    tile = 2 * TILE
    place = (lambda n, rep: (1 - rep[0], n)) if other else (lambda n, rep: (rep[0], n))
    return pl.pallas_call(
        functools.partial(product_body, other, scale, len(panels)),
        grid_spec=pltpu.PrefetchScalarGridSpec(
            num_scalar_prefetch=1,
            grid=(inner // tile,),
            in_specs=[
                pl.BlockSpec((share, rows), lambda n, rep: (0, 0)),
                pl.BlockSpec((share, tile), place),
            ]
            + [pl.BlockSpec((panel.shape[0], tile), lambda n, rep: (0, n)) for panel in panels]
            + [pl.BlockSpec(memory_space=pl.ANY)] * other,
            out_specs=pl.BlockSpec((share, tile), place),
        ),
        out_shape=jax.ShapeDtypeStruct((own, inner), bf16),
        input_output_aliases={3 + len(panels): 0} if other else {},
        compiler_params=pltpu.CompilerParams(vmem_limit_bytes=SMALL if other else LARGE),
        cost_estimate=pl.CostEstimate(flops=2 * share * rows * inner // 3, bytes_accessed=1024, transcendentals=0),
        name="product",
    )(rep, combo, iterate, *panels, *([before] if other else []))


def cut_body(array_ref, out_ref):
    out_ref[...] = array_ref[...]


def cut(array, start, count):
    columns = array.shape[1]
    return pl.pallas_call(
        cut_body,
        grid=(count // TILE,),
        in_specs=[pl.BlockSpec((TILE, columns), lambda t: (start // TILE + t, 0))],
        out_specs=pl.BlockSpec((TILE, columns), lambda t: (t, 0)),
        out_shape=jax.ShapeDtypeStruct((count, columns), array.dtype),
        compiler_params=pltpu.CompilerParams(vmem_limit_bytes=SMALL),
        cost_estimate=cost(2),
        name="cut",
    )(array)


def add_body(parts, array_ref, *refs):
    seconds, whole_ref, outs = refs[:parts], refs[parts], refs[parts + 1 :]
    at = 0
    for ref in seconds:
        rows = pl.ds(at, ref.shape[0])
        whole_ref[rows, :] = (array_ref[rows, :].astype(f32) + ref[...].astype(f32)).astype(bf16)
        at += ref.shape[0]
    at = 0
    for ref in outs:
        ref[...] = whole_ref[pl.ds(at, ref.shape[0]), :]
        at += ref.shape[0]


def add(array, *seconds, split=False):
    shapes = [array.shape] + ([chunk.shape for chunk in jax.eval_shape(chunks, array)] if split else [])
    full = lambda shape: pl.BlockSpec(shape, lambda t: (0, 0))
    return pl.pallas_call(
        functools.partial(add_body, len(seconds)),
        grid=(1,),
        in_specs=[full(x.shape) for x in (array, *seconds)],
        out_specs=[full(shape) for shape in shapes],
        out_shape=[jax.ShapeDtypeStruct(shape, bf16) for shape in shapes],
        compiler_params=pltpu.CompilerParams(vmem_limit_bytes=SMALL),
        cost_estimate=cost(1.5),
        name="add",
    )(array, *seconds)


def chunks(array):
    rows, columns = array.shape
    size = max(TILE, 128 * 1024 // columns // TILE * TILE)
    return [array[at : min(at + size, rows)] for at in range(0, rows, size)]


def local(iterate, sizes):
    own, inner = iterate.shape
    rows = own * sizes["row"]
    cols = inner * sizes["rep"] * sizes["col"]
    share = own // 2
    swap = [(0, 1), (1, 0)]
    rep = lax.axis_index("rep")
    rep_ref = rep.astype(jnp.int32).reshape(1)
    mine_at = rep * share

    widths = piece_widths(own)
    pieces = []
    at = 0
    for width in widths:
        source = iterate if len(pieces) < 2 else tie(iterate, pieces[-2])
        source = cut(source, at, width)
        pieces.append(lax.ppermute(source, "row", swap))
        at += width

    state = {"last": rep_ref}

    def step(function, *args):
        out = function(*tie(args, state["last"]))
        state["last"] = out[-1] if isinstance(out, (tuple, list)) else out
        return out

    class Strip:
        def __init__(self, start, width):
            self.start, self.width = start, width

        def multiply(self, piece, above, offset=0, only=False):
            *sent, self.kept = step(
                lambda piece, *above: strip(rep_ref, piece, iterate, above, self.start, offset, self.width, only),
                piece,
                *above,
            )
            self.taken = [lax.ppermute(chunk, "rep", swap) for chunk in sent]

        def chip(self):
            self.part = step(lambda *a: add(*a)[0], self.kept, *self.taken)
            self.across = lax.ppermute(self.part, "col", swap)

        def total(self, lower=()):
            mine, *self.other = step(
                lambda a, b: add(a, b, split=True), self.part, self.across
            )
            self.mine = [mine, *lower]
            self.other = [lax.ppermute(chunk, "rep", swap) for chunk in self.other]

        def put(self, lower=()):
            before = () if state.get("gram") is None else (state["gram"],)
            parts = len(self.mine)
            arrays = [*self.mine, *self.other, *lower]
            state["gram"] = step(
                lambda *a: put(
                    rep_ref,
                    a[-1] if before else None,
                    rows,
                    self.start,
                    a[:parts],
                    a[parts : len(arrays)],
                ),
                *arrays,
                *before,
            )

    owns, start = [], 0
    for width in own_widths(own):
        item = Strip(start, width)
        item.multiply(iterate, [], start)
        owns.append(item)
        start += width
    for item in owns:
        item.chip()
    others = []
    for width in widths:
        others.append(Strip(start, width))
        start += width

    def arrive(index, before=(), only=False):
        others[index].multiply(pieces[index], pieces[:index], only=only)
        for item in before:
            item.total()
        others[index].chip()
        for item in before:
            item.put()

    def grow(edge, last):
        def widen(gram, *sums):
            return square(rep_ref, gram, sums[0] if sums else None, edge, last, False)

        state["sums"] = step(widen, state["gram"], *([state["sums"]] if edge else []))

    def finish(item):
        item.total()
        item.put()

    arrive(0)
    arrive(1, owns)
    width = widths[-1]
    lower = lax.dynamic_slice(state["gram"], (0, own - width + rep * (width // 2)), (own, width // 2))
    lower = lax.ppermute(tie(lower, pieces[-1]), "row", swap)
    grow(0, own)
    finish(others[0])
    finish(others[1])
    arrive(2)
    grow(own, others[2].start)
    arrive(3, [others[2]], only=True)
    grow(others[2].start, others[3].start)
    last = others[3]
    lower, *lows = step(lambda a: [a, *chunks(a)], lower)
    lows = [lax.ppermute(chunk, "rep", swap) for chunk in lows]
    last.total([lower])
    last.put(lows)
    edge = last.start

    combo = step(lambda gram, sums: square(rep_ref, gram, sums, edge, rows, True), state["gram"], state["sums"])
    scale_factor = 0.2 * math.sqrt(cols)
    theirs = lax.ppermute(combo, "rep", swap)
    result = product(rep_ref, combo, [iterate, *pieces], iterate, None, scale_factor)
    return product(rep_ref, theirs, [iterate, *pieces], iterate, result, scale_factor)


def general(iterate, sizes):
    row_size, rep_size = sizes["row"], sizes["rep"]
    own, inner = iterate.shape
    rows = own * row_size
    cols = inner * rep_size * sizes["col"]
    panel = jnp.concatenate(
        [iterate] + [lax.ppermute(iterate, "row", shift(row_size, by)) for by in range(1, row_size)]
    )
    gram = lax.psum(dot(panel, panel, 1, 1), ("rep", "col")).astype(bf16)
    share = own // rep_size
    mine = lax.dynamic_slice(gram, (0, lax.axis_index("rep") * share), (rows, share))
    combo = (coef_cubic * mine.astype(f32) + coef_quintic * dot(gram, mine, 1, 0)).astype(bf16)
    combo = lax.all_gather(combo, "rep", axis=1, tiled=True)
    scale_factor = 0.2 * jnp.sqrt(f32(cols))
    return (scale_factor * (coef_linear * iterate.astype(f32) + dot(combo, panel, 0, 0))).astype(bf16)


def solution(mesh):
    spec = P(("layer", "row"), ("rep", "col"))
    sizes = dict(mesh.shape)

    def body(iterate):
        pairs = all(sizes[axis] == 2 for axis in ("row", "rep", "col"))
        fits = iterate.shape[0] % TILE == 0 and len(piece_widths(iterate.shape[0])) == 4
        return (local if pairs and fits else general)(iterate, sizes)

    return jax.shard_map(body, mesh=mesh, in_specs=(spec,), out_specs=spec, check_vma=False)
```

```python
import functools
import math

import jax
import jax.numpy as jnp
from jax import lax
from jax.experimental import pallas as pl
from jax.experimental.pallas import tpu as pltpu
from jax.sharding import PartitionSpec as P

coef_linear = 3.4445
coef_cubic = -4.775
coef_quintic = 2.0315

bf16 = jnp.bfloat16
f32 = jnp.float32
TILE = 256
LARGE = 48 * 1024 * 1024
MIDDLE = 40 * 1024 * 1024
SMALL = 28 * 1024 * 1024
SCALE = 0.06e9


def cost(microseconds):
    return pl.CostEstimate(flops=int(microseconds * SCALE), bytes_accessed=1024, transcendentals=0)


def dot(left_side, right_side, left_dim, right_dim):
    return lax.dot_general(
        left_side, right_side, (((left_dim,), (right_dim,)), ((), ())), preferred_element_type=f32
    )


def shift(size, by):
    return [((i + by) % size, i) for i in range(size)]


def rows_of(array, start, count):
    return lax.dynamic_slice(array, (start, 0), (count, array.shape[1]))


def tie(values, after):
    return lax.optimization_barrier((values, after))[0]


def piece_widths(rows):
    units = rows // TILE
    widths = [2 * TILE] * (units // 2)
    return widths[:1] + [TILE] * (units % 2) + widths[1:]


def own_widths(rows):
    units = rows // TILE
    widths = []
    while units > 3:
        widths.append(2 * TILE)
        units -= 2
    return widths + [units * TILE]


def strip_body(start, offset, counts, heights, only, rep_ref, piece_ref, own_ref, *refs):
    above = refs[: len(counts)]
    refs = refs[len(counts) :]
    sents, kept_ref = refs[: len(heights)], refs[len(heights)]
    held, (held_ref, sems) = refs[len(heights) + 1 : -2], refs[-2:]
    width = held_ref.shape[0]
    height = width // 2
    step = pl.program_id(0)
    first = rep_ref[0] == 0
    copies = [pltpu.make_async_copy(piece_ref.at[pl.ds(offset, width), :], held_ref, sems.at[0])]
    copies += [pltpu.make_async_copy(ref, to, sems.at[1 + i]) for i, (ref, to) in enumerate(zip(above, held))]

    @pl.when(step == 0)
    def _():
        for copy in copies:
            copy.start()
        copies[0].wait()

    def store(index, product):
        low, high = product[:, :height], product[:, height:]
        at = sum(heights[:index])
        sents[index][...] = jnp.where(first, high, low).astype(bf16)
        kept_ref[at : at + heights[index], :] = jnp.where(first, low, high).astype(bf16)

    steps = 4 if start else 0
    for index in range(steps):

        @pl.when(step == index)
        def _(index=index):
            store(index, dot(own_ref[...], held_ref[...], 1, 1))

    if not only:

        @pl.when(step == pl.num_programs(0) - 1)
        def _():
            for index, (copy, ref) in enumerate(zip(copies[1:], held)):
                copy.wait()
                store(steps + index, dot(ref[...], held_ref[...], 1, 1))
            store(len(heights) - 1, dot(held_ref[...], held_ref[...], 1, 1))


def strip(rep, piece, iterate, above, start, offset, width, only=False):
    own, inner = iterate.shape
    height = width // 2
    reach = min(start, own)
    tile = reach // 4 if start else 64
    above = [] if only else list(above)
    counts = [array.shape[0] for array in above]
    heights = [tile] * (4 if start else 0) + ([] if only else counts + [width])
    outs = [jax.ShapeDtypeStruct((count, height), bf16) for count in heights + [sum(heights)]]
    any_spec = pl.BlockSpec(memory_space=pl.ANY)
    return pl.pallas_call(
        functools.partial(strip_body, start, offset, counts, heights, only),
        grid=(4 if start else 1,),
        in_specs=[pl.BlockSpec(memory_space=pltpu.SMEM), any_spec, pl.BlockSpec((tile, inner), lambda t: (t, 0))]
        + [any_spec] * len(counts),
        out_specs=[pl.BlockSpec(out.shape, lambda t: (0, 0)) for out in outs],
        out_shape=outs,
        scratch_shapes=[pltpu.VMEM((count, inner), bf16) for count in counts]
        + [pltpu.VMEM((width, inner), bf16), pltpu.SemaphoreType.DMA((1 + len(counts),))],
        compiler_params=pltpu.CompilerParams(vmem_limit_bytes=SMALL),
        cost_estimate=cost(1 + 4 * height * sum(heights) * inner / 0.8e9),
        name="strip",
    )(rep, piece, iterate, *above)


def put_body(start, parts, rep_ref, *refs):
    mines, others = refs[: parts[0]], refs[parts[0] : sum(parts)]
    gram_ref, strip_ref, turned_ref, sems = refs[-4:]
    reach, width = strip_ref.shape
    height = width // 2
    first = rep_ref[0] == 0

    def rows_at(arrays, at):
        for array in arrays:
            if at < array.shape[0]:
                return array[pl.ds(at, TILE), :]
            at -= array.shape[0]

    for at in range(0, reach, TILE):
        there = pl.ds(at, TILE)
        mine, other = rows_at(mines, at), rows_at(others, at)
        low, high = jnp.where(first, mine, other), jnp.where(first, other, mine)
        strip_ref[there, :height] = low
        strip_ref[there, height:] = high
        if at < start:
            turned_ref[:height, there] = low.T
            turned_ref[height:, there] = high.T
    down = pltpu.make_async_copy(strip_ref, gram_ref.at[pl.ds(0, reach), pl.ds(start, width)], sems.at[0])
    down.start()
    if start:
        across = pltpu.make_async_copy(
            turned_ref, gram_ref.at[pl.ds(start, width), pl.ds(0, start)], sems.at[1]
        )
        across.start()
        across.wait()
    down.wait()


def put(rep, gram, rows, start, mines, others):
    height = mines[0].shape[1]
    reach = sum(mine.shape[0] for mine in mines)
    width = 2 * height
    any_spec = pl.BlockSpec(memory_space=pl.ANY)
    first = gram is None
    arrays = [*mines, *others]
    return pl.pallas_call(
        functools.partial(put_body, start, (len(mines), len(others))),
        grid=(1,),
        in_specs=[pl.BlockSpec(memory_space=pltpu.SMEM)]
        + [pl.BlockSpec(array.shape, lambda t: (0, 0)) for array in arrays]
        + ([] if first else [any_spec]),
        out_specs=any_spec,
        out_shape=jax.ShapeDtypeStruct((rows, rows), bf16),
        scratch_shapes=[
            pltpu.VMEM((reach, width), bf16),
            pltpu.VMEM((width, max(start, TILE)), bf16),
            pltpu.SemaphoreType.DMA((2,)),
        ],
        input_output_aliases={} if first else {1 + len(arrays): 0},
        compiler_params=pltpu.CompilerParams(vmem_limit_bytes=LARGE),
        cost_estimate=cost(3),
        name="put",
    )(rep, *arrays, *([] if first else [gram]))


def square_body(edge, last, tile, rep_ref, gram_ref, *refs):
    refs = list(refs)
    base_ref = refs.pop(0) if edge else None
    out_ref, left_ref, thin_ref, tall_ref, sems = refs
    share, reach = left_ref.shape
    old = edge // tile
    step = pl.program_id(0)
    slot = lax.rem(step, 2)
    rows_at = pl.multiple_of(rep_ref[0] * share, 128)

    def left(low, high, sem):
        return pltpu.make_async_copy(
            gram_ref.at[pl.ds(rows_at, share), pl.ds(low, high - low)], left_ref.at[:, pl.ds(low, high - low)], sem
        )

    def thin(step, slot):
        at = pl.ds(pl.multiple_of(step * tile, tile), tile)
        return pltpu.make_async_copy(
            gram_ref.at[pl.ds(edge, reach - edge), at], thin_ref.at[slot], sems.at[2 + slot]
        )

    def tall(step, slot):
        at = pl.ds(pl.multiple_of(step * tile, tile), tile)
        return pltpu.make_async_copy(gram_ref.at[pl.ds(0, reach), at], tall_ref.at[slot], sems.at[4 + slot])

    def start(step, slot):
        if edge:

            @pl.when(step < old)
            def _():
                thin(step, slot).start()

        @pl.when((step >= old) & (step < reach // tile))
        def _():
            tall(step, slot).start()

    parts = [left(at, at + tile, sems.at[6 + at // tile]) for at in range(0, edge, tile)]

    @pl.when(step == 0)
    def _():
        left(edge, reach, sems.at[0]).start()
        start(step, slot)
        for part in parts:
            part.start()
        left(edge, reach, sems.at[0]).wait()

    start(step + 1, 1 - slot)

    def store(total):
        if last:
            near = left_ref[:, pl.ds(pl.multiple_of(step * tile, tile), tile)]
            out_ref[...] = (coef_cubic * near.astype(f32) + coef_quintic * total).astype(bf16)
        else:
            for i in range(tile // TILE):
                out_ref[i] = total[:, i * TILE : (i + 1) * TILE].astype(bf16)

    if edge:

        for index, part in enumerate(parts):

            @pl.when(step == index)
            def _(part=part):
                part.wait()

        @pl.when(step < old)
        def _():
            thin(step, slot).wait()
            base = jnp.concatenate([base_ref[i] for i in range(tile // TILE)], axis=1)
            store(base.astype(f32) + dot(left_ref[:, edge:], thin_ref[slot], 1, 0))

    @pl.when(step >= old)
    def _():
        tall(step, slot).wait()
        store(dot(left_ref[...], tall_ref[slot], 1, 0))


def square(rep, gram, sums, edge, reach, last):
    rows = gram.shape[0]
    share = rows // 4
    wide = 2 * TILE
    tile = TILE if edge % wide or reach % wide else wide
    old = edge // tile
    any_spec = pl.BlockSpec(memory_space=pl.ANY)
    operands, specs = [gram], [any_spec]
    if edge:
        operands.append(sums)
        specs.append(pl.BlockSpec((tile // TILE, share, TILE), lambda n, rep: (jnp.minimum(n, old - 1), 0, 0)))
    if last:
        out, out_spec = (share, rows), pl.BlockSpec((share, tile), lambda n, rep: (0, n))
    else:
        out, out_spec = (rows // TILE, share, TILE), pl.BlockSpec((tile // TILE, share, TILE), lambda n, rep: (n, 0, 0))
    return pl.pallas_call(
        functools.partial(square_body, edge, last, tile),
        grid_spec=pltpu.PrefetchScalarGridSpec(
            num_scalar_prefetch=1,
            grid=(reach // tile,),
            in_specs=specs,
            out_specs=out_spec,
            scratch_shapes=[
                pltpu.VMEM((share, reach), bf16),
                pltpu.VMEM((2, reach - edge if edge else TILE, tile), bf16),
                pltpu.VMEM((2, reach, tile), bf16),
                pltpu.SemaphoreType.DMA((6 + old,)),
            ],
        ),
        out_shape=jax.ShapeDtypeStruct(out, bf16),
        compiler_params=pltpu.CompilerParams(vmem_limit_bytes=MIDDLE if last else LARGE),
        cost_estimate=cost(8 + 5 * share * (edge * (reach - edge) + (reach - edge) * reach) / 0.6e9),
        name="square",
    )(rep, *operands)


def product_body(other, scale, count, rep_ref, combo_ref, linear_ref, *refs):
    out_ref = refs[-1]
    total, at = scale * coef_linear * linear_ref[...].astype(f32), 0
    summed = None
    for ref in refs[:count]:
        rows = ref.shape[0]
        product = dot(combo_ref[:, at : at + rows], ref[...], 1, 0)
        summed = product if summed is None else summed + product
        at += rows
    out_ref[...] = (total + scale * summed).astype(bf16)


def product(rep, combo, panels, iterate, before, scale):
    share, rows = combo.shape
    own, inner = iterate.shape
    other = before is not None
    tile = 2 * TILE
    place = (lambda n, rep: (1 - rep[0], n)) if other else (lambda n, rep: (rep[0], n))
    return pl.pallas_call(
        functools.partial(product_body, other, scale, len(panels)),
        grid_spec=pltpu.PrefetchScalarGridSpec(
            num_scalar_prefetch=1,
            grid=(inner // tile,),
            in_specs=[
                pl.BlockSpec((share, rows), lambda n, rep: (0, 0)),
                pl.BlockSpec((share, tile), place),
            ]
            + [pl.BlockSpec((panel.shape[0], tile), lambda n, rep: (0, n)) for panel in panels]
            + [pl.BlockSpec(memory_space=pl.ANY)] * other,
            out_specs=pl.BlockSpec((share, tile), place),
        ),
        out_shape=jax.ShapeDtypeStruct((own, inner), bf16),
        input_output_aliases={3 + len(panels): 0} if other else {},
        compiler_params=pltpu.CompilerParams(vmem_limit_bytes=MIDDLE),
        cost_estimate=pl.CostEstimate(flops=2 * share * rows * inner // 3, bytes_accessed=1024, transcendentals=0),
        name="product",
    )(rep, combo, iterate, *panels, *([before] if other else []))


def cut_body(array_ref, out_ref):
    out_ref[...] = array_ref[...]


def cut(array, start, count):
    columns = array.shape[1]
    return pl.pallas_call(
        cut_body,
        grid=(count // TILE,),
        in_specs=[pl.BlockSpec((TILE, columns), lambda t: (start // TILE + t, 0))],
        out_specs=pl.BlockSpec((TILE, columns), lambda t: (t, 0)),
        out_shape=jax.ShapeDtypeStruct((count, columns), array.dtype),
        compiler_params=pltpu.CompilerParams(vmem_limit_bytes=SMALL),
        cost_estimate=cost(2),
        name="cut",
    )(array)


def add_body(parts, array_ref, *refs):
    seconds, whole_ref, outs = refs[:parts], refs[parts], refs[parts + 1 :]
    at = 0
    for ref in seconds:
        rows = pl.ds(at, ref.shape[0])
        whole_ref[rows, :] = (array_ref[rows, :].astype(f32) + ref[...].astype(f32)).astype(bf16)
        at += ref.shape[0]
    at = 0
    for ref in outs:
        ref[...] = whole_ref[pl.ds(at, ref.shape[0]), :]
        at += ref.shape[0]


def add(array, *seconds, split=False):
    shapes = [array.shape] + ([chunk.shape for chunk in jax.eval_shape(chunks, array)] if split else [])
    full = lambda shape: pl.BlockSpec(shape, lambda t: (0, 0))
    return pl.pallas_call(
        functools.partial(add_body, len(seconds)),
        grid=(1,),
        in_specs=[full(x.shape) for x in (array, *seconds)],
        out_specs=[full(shape) for shape in shapes],
        out_shape=[jax.ShapeDtypeStruct(shape, bf16) for shape in shapes],
        compiler_params=pltpu.CompilerParams(vmem_limit_bytes=SMALL),
        cost_estimate=cost(1.5),
        name="add",
    )(array, *seconds)


def chunks(array):
    rows, columns = array.shape
    size = max(TILE, 128 * 1024 // columns // TILE * TILE)
    return [array[at : min(at + size, rows)] for at in range(0, rows, size)]


def local(iterate, sizes):
    own, inner = iterate.shape
    rows = own * sizes["row"]
    cols = inner * sizes["rep"] * sizes["col"]
    share = own // 2
    swap = [(0, 1), (1, 0)]
    rep = lax.axis_index("rep")
    rep_ref = rep.astype(jnp.int32).reshape(1)
    mine_at = rep * share

    widths = piece_widths(own)
    pieces = []
    at = 0
    for width in widths:
        source = iterate if len(pieces) < 2 else tie(iterate, pieces[-2])
        source = cut(source, at, width)
        pieces.append(lax.ppermute(source, "row", swap))
        at += width

    state = {"last": rep_ref}

    def step(function, *args):
        out = function(*tie(args, state["last"]))
        state["last"] = out[-1] if isinstance(out, (tuple, list)) else out
        return out

    class Strip:
        def __init__(self, start, width):
            self.start, self.width = start, width

        def multiply(self, piece, above, offset=0, only=False):
            *sent, self.kept = step(
                lambda piece, *above: strip(rep_ref, piece, iterate, above, self.start, offset, self.width, only),
                piece,
                *above,
            )
            self.taken = [lax.ppermute(chunk, "rep", swap) for chunk in sent]

        def chip(self):
            self.part = step(lambda *a: add(*a)[0], self.kept, *self.taken)
            self.across = lax.ppermute(self.part, "col", swap)

        def total(self, lower=()):
            mine, *self.other = step(
                lambda a, b: add(a, b, split=True), self.part, self.across
            )
            self.mine = [mine, *lower]
            self.other = [lax.ppermute(chunk, "rep", swap) for chunk in self.other]

        def put(self, lower=()):
            before = () if state.get("gram") is None else (state["gram"],)
            parts = len(self.mine)
            arrays = [*self.mine, *self.other, *lower]
            state["gram"] = step(
                lambda *a: put(
                    rep_ref,
                    a[-1] if before else None,
                    rows,
                    self.start,
                    a[:parts],
                    a[parts : len(arrays)],
                ),
                *arrays,
                *before,
            )

    owns, start = [], 0
    for width in own_widths(own):
        item = Strip(start, width)
        item.multiply(iterate, [], start)
        owns.append(item)
        start += width
    for item in owns:
        item.chip()
    others = []
    for width in widths:
        others.append(Strip(start, width))
        start += width

    def arrive(index, before=(), only=False):
        others[index].multiply(pieces[index], pieces[:index], only=only)
        if only:
            others[index].chip()
        for item in before:
            item.total()
        if not only:
            others[index].chip()
        for item in before:
            item.put()

    def grow(edge, last):
        def widen(gram, *sums):
            return square(rep_ref, gram, sums[0] if sums else None, edge, last, False)

        state["sums"] = step(widen, state["gram"], *([state["sums"]] if edge else []))

    def finish(item):
        item.total()
        item.put()

    arrive(0)
    arrive(1, owns)
    width = widths[-1]
    lower = lax.dynamic_slice(state["gram"], (0, own - width + rep * (width // 2)), (own, width // 2))
    lower = lax.ppermute(tie(lower, pieces[-1]), "row", swap)
    grow(0, own)
    finish(others[0])
    arrive(2, [others[1]])
    grow(own, others[2].start)
    arrive(3, [others[2]], only=True)
    grow(others[2].start, others[3].start)
    last = others[3]
    lower, *lows = step(lambda a: [a, *chunks(a)], lower)
    lows = [lax.ppermute(chunk, "rep", swap) for chunk in lows]
    last.total([lower])
    last.put(lows)
    edge = last.start

    combo = step(lambda gram, sums: square(rep_ref, gram, sums, edge, rows, True), state["gram"], state["sums"])
    scale_factor = 0.2 * math.sqrt(cols)
    theirs = lax.ppermute(combo, "rep", swap)
    result = product(rep_ref, combo, [iterate, *pieces], iterate, None, scale_factor)
    return product(rep_ref, theirs, [iterate, *pieces], iterate, result, scale_factor)


def general(iterate, sizes):
    row_size, rep_size = sizes["row"], sizes["rep"]
    own, inner = iterate.shape
    rows = own * row_size
    cols = inner * rep_size * sizes["col"]
    panel = jnp.concatenate(
        [iterate] + [lax.ppermute(iterate, "row", shift(row_size, by)) for by in range(1, row_size)]
    )
    gram = lax.psum(dot(panel, panel, 1, 1), ("rep", "col")).astype(bf16)
    share = own // rep_size
    mine = lax.dynamic_slice(gram, (0, lax.axis_index("rep") * share), (rows, share))
    combo = (coef_cubic * mine.astype(f32) + coef_quintic * dot(gram, mine, 1, 0)).astype(bf16)
    combo = lax.all_gather(combo, "rep", axis=1, tiled=True)
    scale_factor = 0.2 * jnp.sqrt(f32(cols))
    return (scale_factor * (coef_linear * iterate.astype(f32) + dot(combo, panel, 0, 0))).astype(bf16)


def solution(mesh):
    spec = P(("layer", "row"), ("rep", "col"))
    sizes = dict(mesh.shape)

    def body(iterate):
        pairs = all(sizes[axis] == 2 for axis in ("row", "rep", "col"))
        fits = iterate.shape[0] % TILE == 0 and len(piece_widths(iterate.shape[0])) == 4
        return (local if pairs and fits else general)(iterate, sizes)

    return jax.shard_map(body, mesh=mesh, in_specs=(spec,), out_specs=spec, check_vma=False)
```

```python
import functools
import math

import jax
import jax.numpy as jnp
from jax import lax
from jax.experimental import pallas as pl
from jax.experimental.pallas import tpu as pltpu
from jax.sharding import PartitionSpec as P

coef_linear = 3.4445
coef_cubic = -4.775
coef_quintic = 2.0315

bf16 = jnp.bfloat16
f32 = jnp.float32
TILE = 256
LARGE = 48 * 1024 * 1024
MIDDLE = 40 * 1024 * 1024
LARGEST = 58 * 1024 * 1024
SMALL = 28 * 1024 * 1024
SCALE = 0.06e9


def cost(microseconds):
    return pl.CostEstimate(flops=int(microseconds * SCALE), bytes_accessed=1024, transcendentals=0)


def dot(left_side, right_side, left_dim, right_dim):
    return lax.dot_general(
        left_side, right_side, (((left_dim,), (right_dim,)), ((), ())), preferred_element_type=f32
    )


def shift(size, by):
    return [((i + by) % size, i) for i in range(size)]


def rows_of(array, start, count):
    return lax.dynamic_slice(array, (start, 0), (count, array.shape[1]))


def tie(values, after):
    return lax.optimization_barrier((values, after))[0]


def piece_widths(rows):
    units = rows // TILE
    widths = [2 * TILE] * (units // 2)
    return widths[:1] + [TILE] * (units % 2) + widths[1:]


def own_widths(rows):
    units = rows // TILE
    widths = []
    while units > 3:
        widths.append(2 * TILE)
        units -= 2
    return widths + [units * TILE]


def strip_body(start, offset, counts, heights, only, rep_ref, piece_ref, own_ref, *refs):
    above = refs[: len(counts)]
    refs = refs[len(counts) :]
    sents, kept_ref = refs[: len(heights)], refs[len(heights)]
    held, (held_ref, sems) = refs[len(heights) + 1 : -2], refs[-2:]
    width = held_ref.shape[0]
    height = width // 2
    step = pl.program_id(0)
    first = rep_ref[0] == 0
    copies = [pltpu.make_async_copy(piece_ref.at[pl.ds(offset, width), :], held_ref, sems.at[0])]
    copies += [pltpu.make_async_copy(ref, to, sems.at[1 + i]) for i, (ref, to) in enumerate(zip(above, held))]

    @pl.when(step == 0)
    def _():
        for copy in copies:
            copy.start()
        copies[0].wait()

    def store(index, product):
        low, high = product[:, :height], product[:, height:]
        at = sum(heights[:index])
        sents[index][...] = jnp.where(first, high, low).astype(bf16)
        kept_ref[at : at + heights[index], :] = jnp.where(first, low, high).astype(bf16)

    steps = 4 if start else 0
    for index in range(steps):

        @pl.when(step == index)
        def _(index=index):
            store(index, dot(own_ref[...], held_ref[...], 1, 1))

    if not only:

        @pl.when(step == pl.num_programs(0) - 1)
        def _():
            for index, (copy, ref) in enumerate(zip(copies[1:], held)):
                copy.wait()
                store(steps + index, dot(ref[...], held_ref[...], 1, 1))
            store(len(heights) - 1, dot(held_ref[...], held_ref[...], 1, 1))


def strip(rep, piece, iterate, above, start, offset, width, only=False):
    own, inner = iterate.shape
    height = width // 2
    reach = min(start, own)
    tile = reach // 4 if start else 64
    above = [] if only else list(above)
    counts = [array.shape[0] for array in above]
    heights = [tile] * (4 if start else 0) + ([] if only else counts + [width])
    outs = [jax.ShapeDtypeStruct((count, height), bf16) for count in heights + [sum(heights)]]
    any_spec = pl.BlockSpec(memory_space=pl.ANY)
    return pl.pallas_call(
        functools.partial(strip_body, start, offset, counts, heights, only),
        grid=(4 if start else 1,),
        in_specs=[pl.BlockSpec(memory_space=pltpu.SMEM), any_spec, pl.BlockSpec((tile, inner), lambda t: (t, 0))]
        + [any_spec] * len(counts),
        out_specs=[pl.BlockSpec(out.shape, lambda t: (0, 0)) for out in outs],
        out_shape=outs,
        scratch_shapes=[pltpu.VMEM((count, inner), bf16) for count in counts]
        + [pltpu.VMEM((width, inner), bf16), pltpu.SemaphoreType.DMA((1 + len(counts),))],
        compiler_params=pltpu.CompilerParams(vmem_limit_bytes=SMALL),
        cost_estimate=cost(1 + 4 * height * sum(heights) * inner / 0.8e9),
        name="strip",
    )(rep, piece, iterate, *above)


def put_body(start, parts, rep_ref, *refs):
    mines, others = refs[: parts[0]], refs[parts[0] : sum(parts)]
    gram_ref, strip_ref, turned_ref, sems = refs[-4:]
    reach, width = strip_ref.shape
    height = width // 2
    first = rep_ref[0] == 0

    def rows_at(arrays, at):
        for array in arrays:
            if at < array.shape[0]:
                return array[pl.ds(at, TILE), :]
            at -= array.shape[0]

    for at in range(0, reach, TILE):
        there = pl.ds(at, TILE)
        mine, other = rows_at(mines, at), rows_at(others, at)
        low, high = jnp.where(first, mine, other), jnp.where(first, other, mine)
        strip_ref[there, :height] = low
        strip_ref[there, height:] = high
        if at < start:
            turned_ref[:height, there] = low.T
            turned_ref[height:, there] = high.T
    down = pltpu.make_async_copy(strip_ref, gram_ref.at[pl.ds(0, reach), pl.ds(start, width)], sems.at[0])
    down.start()
    if start:
        across = pltpu.make_async_copy(
            turned_ref, gram_ref.at[pl.ds(start, width), pl.ds(0, start)], sems.at[1]
        )
        across.start()
        across.wait()
    down.wait()


def put(rep, gram, rows, start, mines, others):
    height = mines[0].shape[1]
    reach = sum(mine.shape[0] for mine in mines)
    width = 2 * height
    any_spec = pl.BlockSpec(memory_space=pl.ANY)
    first = gram is None
    arrays = [*mines, *others]
    return pl.pallas_call(
        functools.partial(put_body, start, (len(mines), len(others))),
        grid=(1,),
        in_specs=[pl.BlockSpec(memory_space=pltpu.SMEM)]
        + [pl.BlockSpec(array.shape, lambda t: (0, 0)) for array in arrays]
        + ([] if first else [any_spec]),
        out_specs=any_spec,
        out_shape=jax.ShapeDtypeStruct((rows, rows), bf16),
        scratch_shapes=[
            pltpu.VMEM((reach, width), bf16),
            pltpu.VMEM((width, max(start, TILE)), bf16),
            pltpu.SemaphoreType.DMA((2,)),
        ],
        input_output_aliases={} if first else {1 + len(arrays): 0},
        compiler_params=pltpu.CompilerParams(vmem_limit_bytes=LARGE),
        cost_estimate=cost(3),
        name="put",
    )(rep, *arrays, *([] if first else [gram]))


def square_body(edge, last, tile, rep_ref, gram_ref, *refs):
    refs = list(refs)
    base_ref = refs.pop(0) if edge else None
    out_ref, left_ref, thin_ref, tall_ref, sems = refs
    share, reach = left_ref.shape
    old = edge // tile
    step = pl.program_id(0)
    slot = lax.rem(step, 2)
    rows_at = pl.multiple_of(rep_ref[0] * share, 128)

    def left(low, high, sem):
        return pltpu.make_async_copy(
            gram_ref.at[pl.ds(rows_at, share), pl.ds(low, high - low)], left_ref.at[:, pl.ds(low, high - low)], sem
        )

    def thin(step, slot):
        at = pl.ds(pl.multiple_of(step * tile, tile), tile)
        return pltpu.make_async_copy(
            gram_ref.at[pl.ds(edge, reach - edge), at], thin_ref.at[slot], sems.at[2 + slot]
        )

    def tall(step, slot):
        at = pl.ds(pl.multiple_of(step * tile, tile), tile)
        return pltpu.make_async_copy(gram_ref.at[pl.ds(0, reach), at], tall_ref.at[slot], sems.at[4 + slot])

    def start(step, slot):
        if edge:

            @pl.when(step < old)
            def _():
                thin(step, slot).start()

        @pl.when((step >= old) & (step < reach // tile))
        def _():
            tall(step, slot).start()

    parts = [left(at, at + tile, sems.at[6 + at // tile]) for at in range(0, edge, tile)]

    @pl.when(step == 0)
    def _():
        left(edge, reach, sems.at[0]).start()
        start(step, slot)
        for part in parts:
            part.start()
        left(edge, reach, sems.at[0]).wait()

    start(step + 1, 1 - slot)

    def store(total):
        if last:
            near = left_ref[:, pl.ds(pl.multiple_of(step * tile, tile), tile)]
            out_ref[...] = (coef_cubic * near.astype(f32) + coef_quintic * total).astype(bf16)
        else:
            for i in range(tile // TILE):
                out_ref[i] = total[:, i * TILE : (i + 1) * TILE].astype(bf16)

    if edge:

        for index, part in enumerate(parts):

            @pl.when(step == index)
            def _(part=part):
                part.wait()

        @pl.when(step < old)
        def _():
            thin(step, slot).wait()
            base = jnp.concatenate([base_ref[i] for i in range(tile // TILE)], axis=1)
            store(base.astype(f32) + dot(left_ref[:, edge:], thin_ref[slot], 1, 0))

    @pl.when(step >= old)
    def _():
        tall(step, slot).wait()
        store(dot(left_ref[...], tall_ref[slot], 1, 0))


def square(rep, gram, sums, edge, reach, last):
    rows = gram.shape[0]
    share = rows // 4
    wide = 2 * TILE
    tile = TILE if edge % wide or reach % wide else wide
    old = edge // tile
    any_spec = pl.BlockSpec(memory_space=pl.ANY)
    operands, specs = [gram], [any_spec]
    if edge:
        operands.append(sums)
        specs.append(pl.BlockSpec((tile // TILE, share, TILE), lambda n, rep: (jnp.minimum(n, old - 1), 0, 0)))
    if last:
        out, out_spec = (share, rows), pl.BlockSpec((share, tile), lambda n, rep: (0, n))
    else:
        out, out_spec = (rows // TILE, share, TILE), pl.BlockSpec((tile // TILE, share, TILE), lambda n, rep: (n, 0, 0))
    return pl.pallas_call(
        functools.partial(square_body, edge, last, tile),
        grid_spec=pltpu.PrefetchScalarGridSpec(
            num_scalar_prefetch=1,
            grid=(reach // tile,),
            in_specs=specs,
            out_specs=out_spec,
            scratch_shapes=[
                pltpu.VMEM((share, reach), bf16),
                pltpu.VMEM((2, reach - edge if edge else TILE, tile), bf16),
                pltpu.VMEM((2, reach, tile), bf16),
                pltpu.SemaphoreType.DMA((6 + old,)),
            ],
        ),
        out_shape=jax.ShapeDtypeStruct(out, bf16),
        compiler_params=pltpu.CompilerParams(vmem_limit_bytes=MIDDLE if last else LARGE),
        cost_estimate=cost(8 + 5 * share * (edge * (reach - edge) + (reach - edge) * reach) / 0.6e9),
        name="square",
    )(rep, *operands)


def product_body(other, scale, count, rep_ref, combo_ref, linear_ref, *refs):
    out_ref = refs[-1]
    total, at = scale * coef_linear * linear_ref[...].astype(f32), 0
    summed = None
    for ref in refs[:count]:
        rows = ref.shape[0]
        product = dot(combo_ref[:, at : at + rows], ref[...], 1, 0)
        summed = product if summed is None else summed + product
        at += rows
    out_ref[...] = (total + scale * summed).astype(bf16)


def product(rep, combo, panels, iterate, before, scale):
    share, rows = combo.shape
    own, inner = iterate.shape
    other = before is not None
    tile = 2 * TILE
    place = (lambda n, rep: (1 - rep[0], n)) if other else (lambda n, rep: (rep[0], n))
    return pl.pallas_call(
        functools.partial(product_body, other, scale, len(panels)),
        grid_spec=pltpu.PrefetchScalarGridSpec(
            num_scalar_prefetch=1,
            grid=(inner // tile,),
            in_specs=[
                pl.BlockSpec((share, rows), lambda n, rep: (0, 0)),
                pl.BlockSpec((share, tile), place),
            ]
            + [pl.BlockSpec((panel.shape[0], tile), lambda n, rep: (0, n)) for panel in panels]
            + [pl.BlockSpec(memory_space=pl.ANY)] * other,
            out_specs=pl.BlockSpec((share, tile), place),
        ),
        out_shape=jax.ShapeDtypeStruct((own, inner), bf16),
        input_output_aliases={3 + len(panels): 0} if other else {},
        compiler_params=pltpu.CompilerParams(vmem_limit_bytes=MIDDLE),
        cost_estimate=pl.CostEstimate(flops=2 * share * rows * inner // 3, bytes_accessed=1024, transcendentals=0),
        name="product",
    )(rep, combo, iterate, *panels, *([before] if other else []))


def cut_body(array_ref, out_ref):
    out_ref[...] = array_ref[...]


def cut(array, start, count):
    columns = array.shape[1]
    return pl.pallas_call(
        cut_body,
        grid=(count // TILE,),
        in_specs=[pl.BlockSpec((TILE, columns), lambda t: (start // TILE + t, 0))],
        out_specs=pl.BlockSpec((TILE, columns), lambda t: (t, 0)),
        out_shape=jax.ShapeDtypeStruct((count, columns), array.dtype),
        compiler_params=pltpu.CompilerParams(vmem_limit_bytes=SMALL if start else LARGEST),
        cost_estimate=cost(2),
        name="cut",
    )(array)


def add_body(parts, array_ref, *refs):
    seconds, whole_ref, outs = refs[:parts], refs[parts], refs[parts + 1 :]
    at = 0
    for ref in seconds:
        rows = pl.ds(at, ref.shape[0])
        whole_ref[rows, :] = (array_ref[rows, :].astype(f32) + ref[...].astype(f32)).astype(bf16)
        at += ref.shape[0]
    at = 0
    for ref in outs:
        ref[...] = whole_ref[pl.ds(at, ref.shape[0]), :]
        at += ref.shape[0]


def add(array, *seconds, split=False):
    shapes = [array.shape] + ([chunk.shape for chunk in jax.eval_shape(chunks, array)] if split else [])
    full = lambda shape: pl.BlockSpec(shape, lambda t: (0, 0))
    return pl.pallas_call(
        functools.partial(add_body, len(seconds)),
        grid=(1,),
        in_specs=[full(x.shape) for x in (array, *seconds)],
        out_specs=[full(shape) for shape in shapes],
        out_shape=[jax.ShapeDtypeStruct(shape, bf16) for shape in shapes],
        compiler_params=pltpu.CompilerParams(vmem_limit_bytes=SMALL),
        cost_estimate=cost(1.5),
        name="add",
    )(array, *seconds)


def chunks(array):
    rows, columns = array.shape
    size = max(TILE, 128 * 1024 // columns // TILE * TILE)
    return [array[at : min(at + size, rows)] for at in range(0, rows, size)]


def local(iterate, sizes):
    own, inner = iterate.shape
    rows = own * sizes["row"]
    cols = inner * sizes["rep"] * sizes["col"]
    share = own // 2
    swap = [(0, 1), (1, 0)]
    rep = lax.axis_index("rep")
    rep_ref = rep.astype(jnp.int32).reshape(1)
    mine_at = rep * share

    widths = piece_widths(own)
    pieces = []
    at = 0
    for width in widths:
        source = iterate if len(pieces) < 2 else tie(iterate, pieces[-2])
        source = cut(source, at, width)
        pieces.append(lax.ppermute(source, "row", swap))
        at += width

    state = {"last": rep_ref}

    def step(function, *args):
        out = function(*tie(args, state["last"]))
        state["last"] = out[-1] if isinstance(out, (tuple, list)) else out
        return out

    class Strip:
        def __init__(self, start, width):
            self.start, self.width = start, width

        def multiply(self, piece, above, offset=0, only=False):
            *sent, self.kept = step(
                lambda piece, *above: strip(rep_ref, piece, iterate, above, self.start, offset, self.width, only),
                piece,
                *above,
            )
            self.taken = [lax.ppermute(chunk, "rep", swap) for chunk in sent]

        def chip(self):
            self.part = step(lambda *a: add(*a)[0], self.kept, *self.taken)
            self.across = lax.ppermute(self.part, "col", swap)

        def total(self, lower=()):
            mine, *self.other = step(
                lambda a, b: add(a, b, split=True), self.part, self.across
            )
            self.mine = [mine, *lower]
            self.other = [lax.ppermute(chunk, "rep", swap) for chunk in self.other]

        def put(self, lower=()):
            before = () if state.get("gram") is None else (state["gram"],)
            parts = len(self.mine)
            arrays = [*self.mine, *self.other, *lower]
            state["gram"] = step(
                lambda *a: put(
                    rep_ref,
                    a[-1] if before else None,
                    rows,
                    self.start,
                    a[:parts],
                    a[parts : len(arrays)],
                ),
                *arrays,
                *before,
            )

    owns, start = [], 0
    for width in own_widths(own):
        item = Strip(start, width)
        item.multiply(iterate, [], start)
        owns.append(item)
        start += width
    for item in owns:
        item.chip()
    others = []
    for width in widths:
        others.append(Strip(start, width))
        start += width

    def arrive(index, before=(), only=False):
        others[index].multiply(pieces[index], pieces[:index], only=only)
        if only:
            others[index].chip()
        for item in before:
            item.total()
        if not only:
            others[index].chip()
        for item in before:
            item.put()

    def grow(edge, last):
        def widen(gram, *sums):
            return square(rep_ref, gram, sums[0] if sums else None, edge, last, False)

        state["sums"] = step(widen, state["gram"], *([state["sums"]] if edge else []))

    def finish(item):
        item.total()
        item.put()

    arrive(0)
    arrive(1, owns)
    width = widths[-1]
    lower = lax.dynamic_slice(state["gram"], (0, own - width + rep * (width // 2)), (own, width // 2))
    lower = lax.ppermute(tie(lower, pieces[-1]), "row", swap)
    grow(0, own)
    finish(others[0])
    arrive(2, [others[1]])
    grow(own, others[2].start)
    arrive(3, [others[2]], only=True)
    grow(others[2].start, others[3].start)
    last = others[3]
    lower, *lows = step(lambda a: [a, *chunks(a)], lower)
    lows = [lax.ppermute(chunk, "rep", swap) for chunk in lows]
    last.total([lower])
    last.put(lows)
    edge = last.start

    combo = step(lambda gram, sums: square(rep_ref, gram, sums, edge, rows, True), state["gram"], state["sums"])
    scale_factor = 0.2 * math.sqrt(cols)
    theirs = lax.ppermute(combo, "rep", swap)
    result = product(rep_ref, combo, [iterate, *pieces], iterate, None, scale_factor)
    return product(rep_ref, theirs, [iterate, *pieces], iterate, result, scale_factor)


def general(iterate, sizes):
    row_size, rep_size = sizes["row"], sizes["rep"]
    own, inner = iterate.shape
    rows = own * row_size
    cols = inner * rep_size * sizes["col"]
    panel = jnp.concatenate(
        [iterate] + [lax.ppermute(iterate, "row", shift(row_size, by)) for by in range(1, row_size)]
    )
    gram = lax.psum(dot(panel, panel, 1, 1), ("rep", "col")).astype(bf16)
    share = own // rep_size
    mine = lax.dynamic_slice(gram, (0, lax.axis_index("rep") * share), (rows, share))
    combo = (coef_cubic * mine.astype(f32) + coef_quintic * dot(gram, mine, 1, 0)).astype(bf16)
    combo = lax.all_gather(combo, "rep", axis=1, tiled=True)
    scale_factor = 0.2 * jnp.sqrt(f32(cols))
    return (scale_factor * (coef_linear * iterate.astype(f32) + dot(combo, panel, 0, 0))).astype(bf16)


def solution(mesh):
    spec = P(("layer", "row"), ("rep", "col"))
    sizes = dict(mesh.shape)

    def body(iterate):
        pairs = all(sizes[axis] == 2 for axis in ("row", "rep", "col"))
        fits = iterate.shape[0] % TILE == 0 and len(piece_widths(iterate.shape[0])) == 4
        return (local if pairs and fits else general)(iterate, sizes)

    return jax.shard_map(body, mesh=mesh, in_specs=(spec,), out_specs=spec, check_vma=False)
```
